32 devices in a mesh: gy: 4 (over z), gz: 8 (over y, x, core).
Axes of the slice: x: 2, y: 2, z: 4, core: 2. Of those that a mesh axis runs over, the one named last changes fastest.
Arguments:
- fields: bfloat16 [1024, 16, 64, 64], P(None, 'gy', 'gz'), may hold values from -6 to 6
- spec_weight: float32 [32, 2, 64, 64], P('gz'), may hold values from -1.5 to 1.5
- skip_weight: bfloat16 [64, 64], replicated, may hold values from -0.75 to 0.75
- up_weight: bfloat16 [64, 256], replicated, may hold values from -0.75 to 0.75
- down_weight: bfloat16 [256, 64], replicated, may hold values from -0.375 to 0.375
- cotangent: bfloat16 [1024, 16, 64, 64], P(None, 'gy', 'gz'), may hold values from -6 to 6
Outputs:
- output: bfloat16 [1024, 16, 64, 64], P(None, 'gy', 'gz')
- grad_fields: bfloat16 [1024, 16, 64, 64], P(None, 'gy', 'gz')
- grad_spec: float32 [32, 2, 64, 64], P('gz')
- grad_skip: float32 [64, 64], replicated
- grad_up: float32 [64, 256], replicated
- grad_down: float32 [256, 64], replicated
The draws below stay inside these ranges and needn't reach their ends.
All inputs are finite; a program needn't handle non-finite values.
Results may differ from the reference program's by a relative error of at most 0.0067.
Values sent between devices are 32-bit elements; how exact they have to be, the bound alone decides.
A program may use at most 192 MiB of HBM per device.

```python
import math
import jax
import jax.numpy as jnp
from jax import lax

NX = 1024
CH = 64
MODES = 32
HID = 256
NY = 16
NZ = 64


def levels(stream_key, shape, split, low, largest):
    def one(dim, parts):
        steps = jax.random.uniform(jax.random.fold_in(jax.random.fold_in(stream_key, 6), dim), (parts,), jnp.float32, low / len(split), largest / len(split))
        return jnp.repeat(jnp.exp(steps), shape[dim] // parts).reshape((-1,) + (1,) * (len(shape) - dim - 1))

    loudness = one(*split[0])
    for cut in split[1:]:
        loudness = loudness * one(*cut)
    return loudness


def gaussian(own_key, dims, width, most, shards=(), kind=jnp.bfloat16):
    values = jax.random.normal(own_key, dims, jnp.float32) * width
    if len(shards) > 0:
        values = levels(own_key, dims, shards, -0.22, 0.18) * values
    return jnp.clip(values, min=-most, max=most).astype(kind)


def setup_inputs(seed: int = 0) -> dict:
    key_list = jax.random.split(jax.random.key(seed), 7)
    return {
        "fields": gaussian(key_list[0], (NX, NY, NZ, CH), 1.0, 6.0, ((1, 4), (2, 8))),
        "spec_weight": gaussian(key_list[1], (MODES, 2, CH, CH), 0.25, 1.5, ((0, 8),), jnp.float32),
        "skip_weight": gaussian(key_list[2], (CH, CH), CH ** -0.5, 0.75),
        "up_weight": gaussian(key_list[3], (CH, HID), CH ** -0.5, 0.75),
        "down_weight": gaussian(key_list[4], (HID, CH), HID ** -0.5, 0.375),
        "cotangent": gaussian(key_list[5], (NX, NY, NZ, CH), 1.0, 6.0, ((1, 4), (2, 8))),
    }


def fourier_tables(length_x, kept):
    position = jnp.arange(length_x, dtype=jnp.int32)[:, None]
    wavenum = jnp.arange(kept, dtype=jnp.int32)[None, :]
    phase = (position * wavenum % length_x).astype(jnp.float32) * (2.0 * math.pi / length_x)
    factor = 1.0 / math.sqrt(length_x)
    analysis = jnp.concatenate([jnp.cos(phase), -jnp.sin(phase)], axis=1) * factor
    doubled = jnp.where(wavenum == 0, 1.0, 2.0).astype(jnp.float32)
    synthesis = jnp.concatenate([jnp.cos(phase) * doubled, -jnp.sin(phase) * doubled], axis=1) * factor
    return (analysis, synthesis)

def to_spectra(stacked, pencils, channels):
    kept = stacked.shape[0] // 2
    return stacked.reshape(2, kept, pencils, channels).transpose(1, 2, 0, 3).reshape(kept, pencils, 2 * channels)

def from_spectra(spectra, channels):
    kept = spectra.shape[0]
    pencils = spectra.shape[1]
    return spectra.reshape(kept, pencils, 2, channels).transpose(2, 0, 1, 3).reshape(2 * kept, pencils * channels)

def mixer_of(weight):
    real_part = weight[:, 0]
    imag_part = weight[:, 1]
    upper = jnp.concatenate([real_part, imag_part], axis=2)
    lower = jnp.concatenate([-imag_part, real_part], axis=2)
    return jnp.concatenate([upper, lower], axis=1)

def weight_grad(moment, channels):
    real_grad = moment[:, :channels, :channels] + moment[:, channels:, channels:]
    imag_grad = moment[:, :channels, channels:] - moment[:, channels:, :channels]
    return jnp.stack([real_grad, imag_grad], axis=1)

def contract_rows(left, right):
    return lax.dot_general(left, right, (((0,), (0,)), ((), ())), preferred_element_type=jnp.float32)

def local_pass(rows_u, rows_s, rows_g, skip_weight, up_weight, down_weight):
    pre_act = rows_s + jnp.dot(rows_u, skip_weight, preferred_element_type=jnp.float32)
    act_full, act_pull = jax.vjp(jax.nn.gelu, pre_act)
    act = act_full.astype(jnp.bfloat16)
    hidden_pre = jnp.dot(act, up_weight, preferred_element_type=jnp.float32)
    hidden_full, hidden_pull = jax.vjp(jax.nn.gelu, hidden_pre)
    hidden = hidden_full.astype(jnp.bfloat16)
    result = jnp.dot(hidden, down_weight, preferred_element_type=jnp.float32).astype(jnp.bfloat16)
    grad_down = contract_rows(hidden, rows_g)
    hidden_cot = jnp.dot(rows_g, down_weight.T, preferred_element_type=jnp.float32)
    hidden_grad = hidden_pull(hidden_cot)[0].astype(jnp.bfloat16)
    grad_up = contract_rows(act, hidden_grad)
    act_cot = jnp.dot(hidden_grad, up_weight.T, preferred_element_type=jnp.float32)
    pre_grad = act_pull(act_cot)[0].astype(jnp.bfloat16)
    grad_skip = contract_rows(rows_u, pre_grad)
    local_cot = jnp.dot(pre_grad, skip_weight.T, preferred_element_type=jnp.float32)
    return (result, pre_grad, local_cot, grad_skip, grad_up, grad_down)

def reference(fields, spec_weight, skip_weight, up_weight, down_weight, cotangent):
    highest = lax.Precision.HIGHEST
    analysis, synthesis = fourier_tables(NX, MODES)
    analysis_low = analysis.astype(jnp.bfloat16)
    synthesis_low = synthesis.astype(jnp.bfloat16)
    by_row = jnp.moveaxis(fields, 1, 0)
    cot_row = jnp.moveaxis(cotangent, 1, 0)

    def forward_row(block):
        flat = block.reshape(NX, NZ * CH)
        return to_spectra(jnp.dot(analysis_low.T, flat, preferred_element_type=jnp.float32), NZ, CH)
    spectra = lax.map(forward_row, by_row)
    mixer = mixer_of(spec_weight)
    mixed = jnp.einsum('ykpi,kio->ykpo', spectra, mixer, precision=highest)

    def middle_row(operands):
        block, mixed_row, cot_block = operands
        field_sum = jnp.dot(synthesis, from_spectra(mixed_row, CH), precision=highest)
        result, pre_grad, local_cot, part_skip, part_up, part_down = local_pass(block.reshape(NX * NZ, CH), field_sum.reshape(NX * NZ, CH), cot_block.reshape(NX * NZ, CH), skip_weight, up_weight, down_weight)
        coeff_grad = to_spectra(jnp.dot(synthesis_low.T, pre_grad.reshape(NX, NZ * CH), preferred_element_type=jnp.float32), NZ, CH)
        return (result.reshape(NX, NZ, CH), local_cot.reshape(NX, NZ * CH), coeff_grad, part_skip, part_up, part_down)
    outputs, local_cots, coeff_grads, skip_parts, up_parts, down_parts = lax.map(middle_row, (by_row, mixed, cot_row))
    moment = jnp.einsum('ykpi,ykpo->kio', spectra, coeff_grads, precision=highest)
    back_spectra = jnp.einsum('ykpo,kio->ykpi', coeff_grads, mixer, precision=highest)

    def final_row(operands):
        local_cot, back_row = operands
        total = local_cot + jnp.dot(analysis, from_spectra(back_row, CH), precision=highest)
        return total.astype(jnp.bfloat16).reshape(NX, NZ, CH)
    grad_rows = lax.map(final_row, (local_cots, back_spectra))
    cell_scale = 1.0 / math.sqrt(NX * NY * NZ)
    pencil_scale = 1.0 / math.sqrt(NY * NZ)
    return (jnp.moveaxis(outputs, 0, 1), jnp.moveaxis(grad_rows, 0, 1), weight_grad(moment, CH) * pencil_scale, lax.optimization_barrier(jnp.sum(skip_parts, axis=0)) * cell_scale, lax.optimization_barrier(jnp.sum(up_parts, axis=0)) * cell_scale, lax.optimization_barrier(jnp.sum(down_parts, axis=0)) * cell_scale)
```

```python
import math

import jax
import jax.numpy as jnp
import numpy as np
from jax import lax
from jax.experimental import pallas as pl
from jax.experimental.pallas import tpu as pltpu
from jax.sharding import PartitionSpec as P

MODES = 32


CHUNK = 256
GELU_SCALE = math.sqrt(2.0 / math.pi)
GELU_CUBE = 0.044715


def fourier_tables(length_x, kept):
    position = np.arange(length_x)[:, None]
    wavenum = np.arange(kept)[None, :]
    phase = (position * wavenum % length_x) * (2.0 * np.pi / length_x)
    factor = 1.0 / math.sqrt(length_x)
    analysis = np.concatenate([np.cos(phase), -np.sin(phase)], axis=1) * factor
    doubled = np.where(wavenum == 0, 1.0, 2.0)
    synthesis = np.concatenate([np.cos(phase) * doubled, -np.sin(phase) * doubled], axis=1) * factor
    return (analysis.astype(np.float32), synthesis.astype(np.float32))


def split_table(table):
    high = table.astype(jnp.bfloat16)
    low = (table - high.astype(np.float32)).astype(jnp.bfloat16)
    return np.concatenate([high.T, high.T, low.T], axis=0)


def split_values(values):
    high = lax.reduce_precision(values, exponent_bits=8, mantissa_bits=7)
    low = (values - high).astype(jnp.bfloat16)
    high = high.astype(jnp.bfloat16)
    return [high, low, high]


def contract_lanes(left, right):
    return lax.dot_general(
        left, right, (((1,), (1,)), ((), ())), preferred_element_type=jnp.float32
    )


def dot(left, right):
    return jnp.dot(left, right, preferred_element_type=jnp.float32)


def gelu_and_slope(x):
    square = x * x
    t = jnp.tanh(x * (GELU_SCALE + (GELU_SCALE * GELU_CUBE) * square))
    half = 0.5 + 0.5 * t
    value = x * half
    slope = half + value * (1.0 - half) * (
        2.0 * GELU_SCALE + (6.0 * GELU_SCALE * GELU_CUBE) * square
    )
    return value, slope


def middle_kernel(
    u_ref, g_ref, coef_ref, table_ref, up_ref, up_t_ref, down_ref, down_t_ref,
    out_ref, pg_ref, both_ref, gup_ref, gdown_ref,
):
    @pl.when(pl.program_id(0) == 0)
    def _():
        gup_ref[...] = jnp.zeros_like(gup_ref)
        gdown_ref[...] = jnp.zeros_like(gdown_ref)

    kept2 = table_ref.shape[0] // 3
    for p in range(u_ref.shape[0]):
        both = 0.0
        gup = 0.0
        gdown = 0.0
        for j in range(u_ref.shape[2] // CHUNK):
            cols = pl.ds(j * CHUNK, CHUNK)
            u = u_ref[p, :, cols]
            g = g_ref[p, :, cols]
            table = table_ref[:, cols]
            pre = dot(coef_ref[p], jnp.concatenate([table, u], axis=0))
            act, act_slope = gelu_and_slope(pre)
            act = act.astype(jnp.bfloat16)
            hidden, hidden_slope = gelu_and_slope(dot(up_t_ref[...], act))
            hidden = hidden.astype(jnp.bfloat16)
            out_ref[p, :, cols] = dot(down_t_ref[...], hidden).astype(jnp.bfloat16)
            hidden_grad = (dot(down_ref[...], g) * hidden_slope).astype(jnp.bfloat16)
            pg = (dot(up_ref[...], hidden_grad) * act_slope).astype(jnp.bfloat16)
            pg_ref[p, :, cols] = pg
            both += contract_lanes(pg, jnp.concatenate([table[:kept2], u], axis=0))
            gdown += contract_lanes(hidden, g)
            gup += contract_lanes(hidden_grad, act)
        both_ref[p] = both
        gup_ref[...] += gup
        gdown_ref[...] += gdown


def final_kernel(pg_ref, coef_ref, table_ref, out_ref):
    for p in range(pg_ref.shape[0]):
        rows = jnp.concatenate([table_ref[...], pg_ref[p]], axis=0)
        out_ref[p] = dot(coef_ref[p], rows).astype(jnp.bfloat16)


def per_pencil(step, rows, cols):
    return pl.BlockSpec((step, rows, cols), lambda i: (i, 0, 0))


def whole(*shape):
    return pl.BlockSpec(shape, lambda i: (0,) * len(shape))


def mixer_of(weight):
    real_part = weight[:, 0]
    imag_part = weight[:, 1]
    upper = jnp.concatenate([real_part, imag_part], axis=2)
    lower = jnp.concatenate([-imag_part, real_part], axis=2)
    return jnp.concatenate([upper, lower], axis=1)


def weight_grad(moment, channels):
    real_grad = moment[:, :channels, :channels] + moment[:, channels:, channels:]
    imag_grad = moment[:, :channels, channels:] - moment[:, channels:, :channels]
    return jnp.stack([real_grad, imag_grad], axis=1)


def mix_modes(spectra, mixer4, channels):
    halves, kept, width = spectra.shape
    pencils = width // channels
    mixed = jnp.einsum(
        "rkpc,krcsd->skpd",
        spectra.reshape(halves, kept, pencils, channels),
        mixer4,
        precision=lax.Precision.HIGHEST,
    )
    return mixed.reshape(halves, kept, width)


def unmix_modes(grads, mixer4, channels):
    halves, kept, width = grads.shape
    pencils = width // channels
    back = jnp.einsum(
        "skpd,krcsd->rkpc",
        grads.reshape(halves, kept, pencils, channels),
        mixer4,
        precision=lax.Precision.HIGHEST,
    )
    return back.reshape(halves, kept, width)


def mode_moment(spectra, grads, channels):
    halves, kept, width = spectra.shape
    pencils = width // channels
    moment = jnp.einsum(
        "rkpc,skpd->krcsd",
        spectra.reshape(halves, kept, pencils, channels),
        grads.reshape(halves, kept, pencils, channels),
        precision=lax.Precision.HIGHEST,
    )
    return moment.reshape(kept, 2 * channels, 2 * channels)


def local(fields, spec_weight, skip_weight, up_weight, down_weight, cotangent):
    length_x, count_y, count_z, channels = fields.shape
    hidden_units = up_weight.shape[1]
    pencils = count_y * count_z
    kept2 = 2 * MODES
    depth = 3 * kept2 + channels
    analysis, synthesis = fourier_tables(length_x, MODES)
    gathered = lax.all_gather(spec_weight, "gz", axis=0, tiled=True)
    u = fields.transpose(1, 2, 3, 0).reshape(pencils, channels, length_x)
    g = cotangent.transpose(1, 2, 3, 0).reshape(pencils, channels, length_x)
    spectra = lax.dot_general(
        jnp.asarray(analysis.astype(jnp.bfloat16)),
        u.reshape(pencils * channels, length_x),
        (((0,), (1,)), ((), ())),
        preferred_element_type=jnp.float32,
    ).reshape(2, MODES, pencils * channels)
    mixer4 = mixer_of(gathered).reshape(MODES, 2, channels, 2, channels)

    def by_pencil(stacked):
        return stacked.reshape(kept2, pencils, channels).transpose(1, 2, 0)

    def with_weight(stacked, weight):
        repeated = jnp.broadcast_to(weight[None], (pencils, channels, channels))
        return jnp.concatenate(split_values(by_pencil(stacked)) + [repeated], axis=2)

    coef = with_weight(mix_modes(spectra, mixer4, channels), skip_weight.T)
    step = 2 if pencils % 2 == 0 else 1
    result, pre_grad, both, gup, gdown = pl.pallas_call(
        middle_kernel,
        grid=(pencils // step,),
        in_specs=[
            per_pencil(step, channels, length_x),
            per_pencil(step, channels, length_x),
            per_pencil(step, channels, depth),
            whole(3 * kept2, length_x),
            whole(channels, hidden_units),
            whole(hidden_units, channels),
            whole(hidden_units, channels),
            whole(channels, hidden_units),
        ],
        out_specs=[
            per_pencil(step, channels, length_x),
            per_pencil(step, channels, length_x),
            per_pencil(step, channels, kept2 + channels),
            whole(hidden_units, channels),
            whole(hidden_units, channels),
        ],
        out_shape=[
            jax.ShapeDtypeStruct((pencils, channels, length_x), jnp.bfloat16),
            jax.ShapeDtypeStruct((pencils, channels, length_x), jnp.bfloat16),
            jax.ShapeDtypeStruct((pencils, channels, kept2 + channels), jnp.float32),
            jax.ShapeDtypeStruct((hidden_units, channels), jnp.float32),
            jax.ShapeDtypeStruct((hidden_units, channels), jnp.float32),
        ],
        compiler_params=pltpu.CompilerParams(vmem_limit_bytes=40 * 1024 * 1024),
        name="middle",
    )(
        u, g, coef, jnp.asarray(split_table(synthesis)),
        up_weight, up_weight.T, down_weight, down_weight.T,
    )
    gskip = jnp.sum(both[:, :, kept2:], axis=0).T
    coeff_grads = both[:, :, :kept2].transpose(2, 0, 1).reshape(2, MODES, pencils * channels)
    moment = mode_moment(spectra, coeff_grads, channels)
    owned_share = lax.psum_scatter(
        weight_grad(moment, channels), "gz", scatter_dimension=0, tiled=True
    )
    spec_total = lax.psum(owned_share, "gy")
    packed = lax.psum(jnp.concatenate([gdown, gup, gskip], axis=0), ("gy", "gz"))
    back = with_weight(unmix_modes(coeff_grads, mixer4, channels), skip_weight)
    grad_fields = pl.pallas_call(
        final_kernel,
        grid=(pencils // step,),
        in_specs=[
            per_pencil(step, channels, length_x),
            per_pencil(step, channels, depth),
            whole(3 * kept2, length_x),
        ],
        out_specs=per_pencil(step, channels, length_x),
        out_shape=jax.ShapeDtypeStruct((pencils, channels, length_x), jnp.bfloat16),
        compiler_params=pltpu.CompilerParams(vmem_limit_bytes=40 * 1024 * 1024),
        name="final",
    )(pre_grad, back, jnp.asarray(split_table(analysis)))
    all_pencils = pencils * lax.axis_size("gy") * lax.axis_size("gz")
    cell_scale = 1.0 / math.sqrt(length_x * all_pencils)
    pencil_scale = 1.0 / math.sqrt(all_pencils)

    def to_grid(rows):
        return rows.reshape(count_y, count_z, channels, length_x).transpose(3, 0, 1, 2)

    return (
        to_grid(result),
        to_grid(grad_fields),
        spec_total * pencil_scale,
        packed[2 * hidden_units :] * cell_scale,
        packed[hidden_units : 2 * hidden_units].T * cell_scale,
        packed[:hidden_units] * cell_scale,
    )


def solution(mesh):
    placed = (
        P(None, "gy", "gz", None),
        P("gz", None, None, None),
        P(),
        P(),
        P(),
        P(None, "gy", "gz", None),
    )
    return jax.shard_map(
        local,
        mesh=mesh,
        in_specs=placed,
        out_specs=(
            P(None, "gy", "gz", None),
            P(None, "gy", "gz", None),
            P("gz", None, None, None),
            P(),
            P(),
            P(),
        ),
        check_vma=False,
    )
```

```python
import math

import jax
import jax.numpy as jnp
import numpy as np
from jax import lax
from jax.experimental import pallas as pl
from jax.experimental.pallas import tpu as pltpu
from jax.sharding import PartitionSpec as P

MODES = 32


CHUNK = 256
GELU_SCALE = math.sqrt(2.0 / math.pi)
GELU_CUBE = 0.044715


def fourier_tables(length_x, kept):
    position = np.arange(length_x)[:, None]
    wavenum = np.arange(kept)[None, :]
    phase = (position * wavenum % length_x) * (2.0 * np.pi / length_x)
    factor = 1.0 / math.sqrt(length_x)
    analysis = np.concatenate([np.cos(phase), -np.sin(phase)], axis=1) * factor
    doubled = np.where(wavenum == 0, 1.0, 2.0)
    synthesis = np.concatenate([np.cos(phase) * doubled, -np.sin(phase) * doubled], axis=1) * factor
    return (analysis.astype(np.float32), synthesis.astype(np.float32))


def split_table(table):
    high = table.astype(jnp.bfloat16)
    low = (table - high.astype(np.float32)).astype(jnp.bfloat16)
    return np.concatenate([high.T, high.T, low.T], axis=0)


def split_values(values):
    high = lax.reduce_precision(values, exponent_bits=8, mantissa_bits=7)
    low = (values - high).astype(jnp.bfloat16)
    high = high.astype(jnp.bfloat16)
    return [high, low, high]


def contract_lanes(left, right):
    return lax.dot_general(
        left, right, (((1,), (1,)), ((), ())), preferred_element_type=jnp.float32
    )


def dot(left, right):
    return jnp.dot(left, right, preferred_element_type=jnp.float32)


def gelu_and_slope(x):
    square = x * x
    t = jnp.tanh(x * (GELU_SCALE + (GELU_SCALE * GELU_CUBE) * square))
    half = 0.5 + 0.5 * t
    value = x * half
    slope = half + value * (1.0 - half) * (
        2.0 * GELU_SCALE + (6.0 * GELU_SCALE * GELU_CUBE) * square
    )
    return value, slope


def middle_kernel(
    u_ref, g_ref, coef_ref, table_ref, up_ref, up_t_ref, down_ref, down_t_ref,
    out_ref, pg_ref, both_ref, gup_ref, gdown_ref,
):
    @pl.when(pl.program_id(0) == 0)
    def _():
        gup_ref[...] = jnp.zeros_like(gup_ref)
        gdown_ref[...] = jnp.zeros_like(gdown_ref)

    kept2 = table_ref.shape[0] // 3
    for p in range(u_ref.shape[0]):
        both = 0.0
        gup = 0.0
        gdown = 0.0
        for j in range(u_ref.shape[2] // CHUNK):
            cols = pl.ds(j * CHUNK, CHUNK)
            u = u_ref[p, :, cols]
            g = g_ref[p, :, cols]
            table = table_ref[:, cols]
            pre = dot(coef_ref[p], jnp.concatenate([table, u], axis=0))
            act, act_slope = gelu_and_slope(pre)
            act = act.astype(jnp.bfloat16)
            hidden, hidden_slope = gelu_and_slope(dot(up_t_ref[...], act))
            hidden = hidden.astype(jnp.bfloat16)
            out_ref[p, :, cols] = dot(down_t_ref[...], hidden).astype(jnp.bfloat16)
            hidden_grad = (dot(down_ref[...], g) * hidden_slope).astype(jnp.bfloat16)
            pg = (dot(up_ref[...], hidden_grad) * act_slope).astype(jnp.bfloat16)
            pg_ref[p, :, cols] = pg
            both += contract_lanes(pg, jnp.concatenate([table[:kept2], u], axis=0))
            gdown += contract_lanes(hidden, g)
            gup += contract_lanes(hidden_grad, act)
        both_ref[p] = both
        gup_ref[...] += gup
        gdown_ref[...] += gdown


def final_kernel(pg_ref, coef_ref, table_ref, out_ref):
    for p in range(pg_ref.shape[0]):
        rows = jnp.concatenate([table_ref[...], pg_ref[p]], axis=0)
        out_ref[p] = dot(coef_ref[p], rows).astype(jnp.bfloat16)


def per_pencil(step, rows, cols):
    return pl.BlockSpec((step, rows, cols), lambda i: (i, 0, 0))


def whole(*shape):
    return pl.BlockSpec(shape, lambda i: (0,) * len(shape))


def mixer_of(weight):
    real_part = weight[:, 0]
    imag_part = weight[:, 1]
    upper = jnp.concatenate([real_part, imag_part], axis=2)
    lower = jnp.concatenate([-imag_part, real_part], axis=2)
    return jnp.concatenate([upper, lower], axis=1)


def weight_grad(moment, channels):
    real_grad = moment[:, :channels, :channels] + moment[:, channels:, channels:]
    imag_grad = moment[:, :channels, channels:] - moment[:, channels:, :channels]
    return jnp.stack([real_grad, imag_grad], axis=1)


def mix_modes(spectra, mixer4, channels):
    halves, kept, width = spectra.shape
    pencils = width // channels
    mixed = jnp.einsum(
        "rkpc,krcsd->skpd",
        spectra.reshape(halves, kept, pencils, channels),
        mixer4,
        precision=lax.Precision.HIGHEST,
    )
    return mixed.reshape(halves, kept, width)


def unmix_modes(grads, mixer4, channels):
    halves, kept, width = grads.shape
    pencils = width // channels
    back = jnp.einsum(
        "skpd,krcsd->rkpc",
        grads.reshape(halves, kept, pencils, channels),
        mixer4,
        precision=lax.Precision.HIGHEST,
    )
    return back.reshape(halves, kept, width)


def mode_moment(spectra, grads, channels):
    halves, kept, width = spectra.shape
    pencils = width // channels
    moment = jnp.einsum(
        "rkpc,skpd->krcsd",
        spectra.reshape(halves, kept, pencils, channels),
        grads.reshape(halves, kept, pencils, channels),
        precision=lax.Precision.HIGHEST,
    )
    return moment.reshape(kept, 2 * channels, 2 * channels)


def local(fields, spec_weight, skip_weight, up_weight, down_weight, cotangent):
    length_x, count_y, count_z, channels = fields.shape
    hidden_units = up_weight.shape[1]
    pencils = count_y * count_z
    kept2 = 2 * MODES
    depth = 3 * kept2 + channels
    analysis, synthesis = fourier_tables(length_x, MODES)
    gathered = lax.all_gather(spec_weight, "gz", axis=0, tiled=True)
    u = fields.transpose(1, 2, 3, 0).reshape(pencils, channels, length_x)
    g = cotangent.transpose(1, 2, 3, 0).reshape(pencils, channels, length_x)
    spectra = lax.dot_general(
        jnp.asarray(analysis.astype(jnp.bfloat16)),
        u.reshape(pencils * channels, length_x),
        (((0,), (1,)), ((), ())),
        preferred_element_type=jnp.float32,
    ).reshape(2, MODES, pencils * channels)
    mixer4 = mixer_of(gathered).reshape(MODES, 2, channels, 2, channels)

    def by_pencil(stacked):
        return stacked.reshape(kept2, pencils, channels).transpose(1, 2, 0)

    def with_weight(stacked, weight):
        repeated = jnp.broadcast_to(weight[None], (pencils, channels, channels))
        return jnp.concatenate(split_values(by_pencil(stacked)) + [repeated], axis=2)

    coef = with_weight(mix_modes(spectra, mixer4, channels), skip_weight.T)
    step = 2 if pencils % 2 == 0 else 1
    result, pre_grad, both, gup, gdown = pl.pallas_call(
        middle_kernel,
        grid=(pencils // step,),
        in_specs=[
            per_pencil(step, channels, length_x),
            per_pencil(step, channels, length_x),
            per_pencil(step, channels, depth),
            whole(3 * kept2, length_x),
            whole(channels, hidden_units),
            whole(hidden_units, channels),
            whole(hidden_units, channels),
            whole(channels, hidden_units),
        ],
        out_specs=[
            per_pencil(step, channels, length_x),
            per_pencil(step, channels, length_x),
            per_pencil(step, channels, kept2 + channels),
            whole(hidden_units, channels),
            whole(hidden_units, channels),
        ],
        out_shape=[
            jax.ShapeDtypeStruct((pencils, channels, length_x), jnp.bfloat16),
            jax.ShapeDtypeStruct((pencils, channels, length_x), jnp.bfloat16),
            jax.ShapeDtypeStruct((pencils, channels, kept2 + channels), jnp.float32),
            jax.ShapeDtypeStruct((hidden_units, channels), jnp.float32),
            jax.ShapeDtypeStruct((hidden_units, channels), jnp.float32),
        ],
        compiler_params=pltpu.CompilerParams(vmem_limit_bytes=40 * 1024 * 1024),
        name="middle",
    )(
        u, g, coef, jnp.asarray(split_table(synthesis)),
        up_weight, up_weight.T, down_weight, down_weight.T,
    )
    gskip = jnp.sum(both[:, :, kept2:], axis=0).T
    coeff_grads = both[:, :, :kept2].transpose(2, 0, 1).reshape(2, MODES, pencils * channels)
    moment = mode_moment(spectra, coeff_grads, channels)
    owners = lax.axis_size("gz")
    spec_part = weight_grad(moment, channels).reshape(owners, -1, 128)
    packed_part = jnp.concatenate([gdown, gup, gskip], axis=0).reshape(owners, -1, 128)
    spec_rows = spec_part.shape[1]
    shares = lax.all_to_all(
        jnp.concatenate([spec_part, packed_part], axis=1), "gz", 0, 0, tiled=True
    )
    owned = jnp.sum(lax.all_gather(jnp.sum(shares, axis=0), "gy", axis=0), axis=0)
    spec_total = owned[:spec_rows].reshape(spec_weight.shape)
    packed = lax.all_gather(owned[spec_rows:], "gz", axis=0).reshape(-1, channels)
    back = with_weight(unmix_modes(coeff_grads, mixer4, channels), skip_weight)
    grad_fields = pl.pallas_call(
        final_kernel,
        grid=(pencils // step,),
        in_specs=[
            per_pencil(step, channels, length_x),
            per_pencil(step, channels, depth),
            whole(3 * kept2, length_x),
        ],
        out_specs=per_pencil(step, channels, length_x),
        out_shape=jax.ShapeDtypeStruct((pencils, channels, length_x), jnp.bfloat16),
        compiler_params=pltpu.CompilerParams(vmem_limit_bytes=40 * 1024 * 1024),
        name="final",
    )(pre_grad, back, jnp.asarray(split_table(analysis)))
    all_pencils = pencils * lax.axis_size("gy") * lax.axis_size("gz")
    cell_scale = 1.0 / math.sqrt(length_x * all_pencils)
    pencil_scale = 1.0 / math.sqrt(all_pencils)

    def to_grid(rows):
        return rows.reshape(count_y, count_z, channels, length_x).transpose(3, 0, 1, 2)

    return (
        to_grid(result),
        to_grid(grad_fields),
        spec_total * pencil_scale,
        packed[2 * hidden_units :] * cell_scale,
        packed[hidden_units : 2 * hidden_units].T * cell_scale,
        packed[:hidden_units] * cell_scale,
    )


def solution(mesh):
    placed = (
        P(None, "gy", "gz", None),
        P("gz", None, None, None),
        P(),
        P(),
        P(),
        P(None, "gy", "gz", None),
    )
    return jax.shard_map(
        local,
        mesh=mesh,
        in_specs=placed,
        out_specs=(
            P(None, "gy", "gz", None),
            P(None, "gy", "gz", None),
            P("gz", None, None, None),
            P(),
            P(),
            P(),
        ),
        check_vma=False,
    )
```

```python
import math

import jax
import jax.numpy as jnp
import numpy as np
from jax import lax
from jax.experimental import pallas as pl
from jax.experimental.pallas import tpu as pltpu
from jax.sharding import PartitionSpec as P

MODES = 32


CHUNK = 512
GELU_SCALE = math.sqrt(2.0 / math.pi)
GELU_CUBE = 0.044715


def fourier_tables(length_x, kept):
    position = np.arange(length_x)[:, None]
    wavenum = np.arange(kept)[None, :]
    phase = (position * wavenum % length_x) * (2.0 * np.pi / length_x)
    factor = 1.0 / math.sqrt(length_x)
    analysis = np.concatenate([np.cos(phase), -np.sin(phase)], axis=1) * factor
    doubled = np.where(wavenum == 0, 1.0, 2.0)
    synthesis = np.concatenate([np.cos(phase) * doubled, -np.sin(phase) * doubled], axis=1) * factor
    return (analysis.astype(np.float32), synthesis.astype(np.float32))


def split_table(table):
    high = table.astype(jnp.bfloat16)
    low = (table - high.astype(np.float32)).astype(jnp.bfloat16)
    return np.concatenate([high.T, high.T, low.T], axis=0)


def split_values(values):
    high = lax.reduce_precision(values, exponent_bits=8, mantissa_bits=7)
    low = (values - high).astype(jnp.bfloat16)
    high = high.astype(jnp.bfloat16)
    return [high, low, high]


def contract_lanes(left, right):
    return lax.dot_general(
        left, right, (((1,), (1,)), ((), ())), preferred_element_type=jnp.float32
    )


def dot(left, right):
    return jnp.dot(left, right, preferred_element_type=jnp.float32)


def gelu_and_slope(x):
    square = x * x
    t = jnp.tanh(x * (GELU_SCALE + (GELU_SCALE * GELU_CUBE) * square))
    half = 0.5 + 0.5 * t
    value = x * half
    slope = half + value * (1.0 - half) * (
        2.0 * GELU_SCALE + (6.0 * GELU_SCALE * GELU_CUBE) * square
    )
    return value, slope


def middle_kernel(
    u_ref, g_ref, coef_ref, table_ref, up_ref, up_t_ref, down_ref, down_t_ref,
    out_ref, pg_ref, both_ref, gup_ref, gdown_ref,
):
    @pl.when(pl.program_id(0) == 0)
    def _():
        gup_ref[...] = jnp.zeros_like(gup_ref)
        gdown_ref[...] = jnp.zeros_like(gdown_ref)

    kept2 = table_ref.shape[0] // 3
    for p in range(u_ref.shape[0]):
        both = 0.0
        gup = 0.0
        gdown = 0.0
        for j in range(u_ref.shape[2] // CHUNK):
            cols = pl.ds(j * CHUNK, CHUNK)
            u = u_ref[p, :, cols]
            g = g_ref[p, :, cols]
            table = table_ref[:, cols]
            pre = dot(coef_ref[p], jnp.concatenate([table, u], axis=0))
            act, act_slope = gelu_and_slope(pre)
            act = act.astype(jnp.bfloat16)
            hidden, hidden_slope = gelu_and_slope(dot(up_t_ref[...], act))
            hidden = hidden.astype(jnp.bfloat16)
            out_ref[p, :, cols] = dot(down_t_ref[...], hidden).astype(jnp.bfloat16)
            hidden_grad = (dot(down_ref[...], g) * hidden_slope).astype(jnp.bfloat16)
            pg = (dot(up_ref[...], hidden_grad) * act_slope).astype(jnp.bfloat16)
            pg_ref[p, :, cols] = pg
            both += contract_lanes(pg, jnp.concatenate([table[:kept2], u], axis=0))
            gdown += contract_lanes(hidden, g)
            gup += contract_lanes(hidden_grad, act)
        both_ref[p] = both
        gup_ref[...] += gup
        gdown_ref[...] += gdown


def final_kernel(pg_ref, coef_ref, table_ref, out_ref):
    for p in range(pg_ref.shape[0]):
        rows = jnp.concatenate([table_ref[...], pg_ref[p]], axis=0)
        out_ref[p] = dot(coef_ref[p], rows).astype(jnp.bfloat16)


def per_pencil(step, rows, cols):
    return pl.BlockSpec((step, rows, cols), lambda i: (i, 0, 0))


def whole(*shape):
    return pl.BlockSpec(shape, lambda i: (0,) * len(shape))


def mixer_of(weight):
    real_part = weight[:, 0]
    imag_part = weight[:, 1]
    upper = jnp.concatenate([real_part, imag_part], axis=2)
    lower = jnp.concatenate([-imag_part, real_part], axis=2)
    return jnp.concatenate([upper, lower], axis=1)


def weight_grad(moment, channels):
    real_grad = moment[:, :channels, :channels] + moment[:, channels:, channels:]
    imag_grad = moment[:, :channels, channels:] - moment[:, channels:, :channels]
    return jnp.stack([real_grad, imag_grad], axis=1)


def mix_modes(spectra, mixer4, channels):
    halves, kept, width = spectra.shape
    pencils = width // channels
    mixed = jnp.einsum(
        "rkpc,krcsd->skpd",
        spectra.reshape(halves, kept, pencils, channels),
        mixer4,
        precision=lax.Precision.HIGHEST,
    )
    return mixed.reshape(halves, kept, width)


def unmix_modes(grads, mixer4, channels):
    halves, kept, width = grads.shape
    pencils = width // channels
    back = jnp.einsum(
        "skpd,krcsd->rkpc",
        grads.reshape(halves, kept, pencils, channels),
        mixer4,
        precision=lax.Precision.HIGHEST,
    )
    return back.reshape(halves, kept, width)


def mode_moment(spectra, grads, channels):
    halves, kept, width = spectra.shape
    pencils = width // channels
    moment = jnp.einsum(
        "rkpc,skpd->krcsd",
        spectra.reshape(halves, kept, pencils, channels),
        grads.reshape(halves, kept, pencils, channels),
        precision=lax.Precision.HIGHEST,
    )
    return moment.reshape(kept, 2 * channels, 2 * channels)


def local(fields, spec_weight, skip_weight, up_weight, down_weight, cotangent):
    length_x, count_y, count_z, channels = fields.shape
    hidden_units = up_weight.shape[1]
    pencils = count_y * count_z
    kept2 = 2 * MODES
    depth = 3 * kept2 + channels
    analysis, synthesis = fourier_tables(length_x, MODES)
    gathered = lax.all_gather(spec_weight, "gz", axis=0, tiled=True)
    u = fields.transpose(1, 2, 3, 0).reshape(pencils, channels, length_x)
    g = cotangent.transpose(1, 2, 3, 0).reshape(pencils, channels, length_x)
    spectra = lax.dot_general(
        jnp.asarray(analysis.astype(jnp.bfloat16)),
        u.reshape(pencils * channels, length_x),
        (((0,), (1,)), ((), ())),
        preferred_element_type=jnp.float32,
    ).reshape(2, MODES, pencils * channels)
    mixer4 = mixer_of(gathered).reshape(MODES, 2, channels, 2, channels)

    def by_pencil(stacked):
        return stacked.reshape(kept2, pencils, channels).transpose(1, 2, 0)

    def with_weight(stacked, weight):
        repeated = jnp.broadcast_to(weight[None], (pencils, channels, channels))
        return jnp.concatenate(split_values(by_pencil(stacked)) + [repeated], axis=2)

    coef = with_weight(mix_modes(spectra, mixer4, channels), skip_weight.T)
    step = 2 if pencils % 2 == 0 else 1
    result, pre_grad, both, gup, gdown = pl.pallas_call(
        middle_kernel,
        grid=(pencils // step,),
        in_specs=[
            per_pencil(step, channels, length_x),
            per_pencil(step, channels, length_x),
            per_pencil(step, channels, depth),
            whole(3 * kept2, length_x),
            whole(channels, hidden_units),
            whole(hidden_units, channels),
            whole(hidden_units, channels),
            whole(channels, hidden_units),
        ],
        out_specs=[
            per_pencil(step, channels, length_x),
            per_pencil(step, channels, length_x),
            per_pencil(step, channels, kept2 + channels),
            whole(hidden_units, channels),
            whole(hidden_units, channels),
        ],
        out_shape=[
            jax.ShapeDtypeStruct((pencils, channels, length_x), jnp.bfloat16),
            jax.ShapeDtypeStruct((pencils, channels, length_x), jnp.bfloat16),
            jax.ShapeDtypeStruct((pencils, channels, kept2 + channels), jnp.float32),
            jax.ShapeDtypeStruct((hidden_units, channels), jnp.float32),
            jax.ShapeDtypeStruct((hidden_units, channels), jnp.float32),
        ],
        compiler_params=pltpu.CompilerParams(vmem_limit_bytes=40 * 1024 * 1024),
        name="middle",
    )(
        u, g, coef, jnp.asarray(split_table(synthesis)),
        up_weight, up_weight.T, down_weight, down_weight.T,
    )
    gskip = jnp.sum(both[:, :, kept2:], axis=0).T
    coeff_grads = both[:, :, :kept2].transpose(2, 0, 1).reshape(2, MODES, pencils * channels)
    moment = mode_moment(spectra, coeff_grads, channels)
    owners = lax.axis_size("gz")
    spec_part = weight_grad(moment, channels).reshape(owners, -1, 128)
    packed_part = jnp.concatenate([gdown, gup, gskip], axis=0).reshape(owners, -1, 128)
    spec_rows = spec_part.shape[1]
    shares = lax.all_to_all(
        jnp.concatenate([spec_part, packed_part], axis=1), "gz", 0, 0, tiled=True
    )
    owned = jnp.sum(lax.all_gather(jnp.sum(shares, axis=0), "gy", axis=0), axis=0)
    spec_total = owned[:spec_rows].reshape(spec_weight.shape)
    packed = lax.all_gather(owned[spec_rows:], "gz", axis=0).reshape(-1, channels)
    back = with_weight(unmix_modes(coeff_grads, mixer4, channels), skip_weight)
    grad_fields = pl.pallas_call(
        final_kernel,
        grid=(pencils // step,),
        in_specs=[
            per_pencil(step, channels, length_x),
            per_pencil(step, channels, depth),
            whole(3 * kept2, length_x),
        ],
        out_specs=per_pencil(step, channels, length_x),
        out_shape=jax.ShapeDtypeStruct((pencils, channels, length_x), jnp.bfloat16),
        compiler_params=pltpu.CompilerParams(vmem_limit_bytes=40 * 1024 * 1024),
        name="final",
    )(pre_grad, back, jnp.asarray(split_table(analysis)))
    all_pencils = pencils * lax.axis_size("gy") * lax.axis_size("gz")
    cell_scale = 1.0 / math.sqrt(length_x * all_pencils)
    pencil_scale = 1.0 / math.sqrt(all_pencils)

    def to_grid(rows):
        return rows.reshape(count_y, count_z, channels, length_x).transpose(3, 0, 1, 2)

    return (
        to_grid(result),
        to_grid(grad_fields),
        spec_total * pencil_scale,
        packed[2 * hidden_units :] * cell_scale,
        packed[hidden_units : 2 * hidden_units].T * cell_scale,
        packed[:hidden_units] * cell_scale,
    )


def solution(mesh):
    placed = (
        P(None, "gy", "gz", None),
        P("gz", None, None, None),
        P(),
        P(),
        P(),
        P(None, "gy", "gz", None),
    )
    return jax.shard_map(
        local,
        mesh=mesh,
        in_specs=placed,
        out_specs=(
            P(None, "gy", "gz", None),
            P(None, "gy", "gz", None),
            P("gz", None, None, None),
            P(),
            P(),
            P(),
        ),
        check_vma=False,
    )
```
